128 devices in a mesh: prow: 8 (over x, core), pcol: 16 (over y, z).
Axes of the slice: x: 4, y: 4, z: 4, core: 2. Of those that a mesh axis runs over, the one named last changes fastest.
Arguments:
- samples: float32 [16384, 64], P(('prow', 'pcol'))
- position: int32 [16384], P(('prow', 'pcol')), may hold values from 0 to 16383, as said below
- slot_of_block: int32 [64], replicated, may hold values from 0 to 63, as said below
- structure: int32 [64, 64], replicated, may hold values from 0 to 1, as said below
Outputs:
- panel: float32 [16384, 512], P('prow')
- trailing: float32 [16384, 16384], P('prow', 'pcol')
The draws below stay inside these ranges and needn't reach their ends.
Inputs may be any that keep to these rules, and one draw needn't show every extreme that they name: A permutation. A sample at position p, in block p div 256 with slot s, is destined for the device at grid row s mod (devices along prow) and grid column (p mod 256) div (256 / devices along pcol). No device holds more than 2 samples for one destination; every device holds exactly 2 for some destination and is the destination of exactly 2 samples from some device; every device is the destination of exactly 128 samples. `slot_of_block`: A permutation. `structure`: Symmetric, with ones on the diagonal.
All inputs are finite; a program needn't handle non-finite values.
Results may differ from the reference program's by a relative error of at most 0.0003.
Values sent between devices are 32-bit elements; how exact they have to be, the bound alone decides.
A program may use at most 128 MiB of HBM per device.

```python
import math
import jax
import jax.numpy as jnp
from jax import lax

BLOCK = 256
FEAT = 64
NB = 64
N = 16384
SRC = 128
CAP = 2
N_PROW = 8
N_PCOL = 16
DEVICES = 128


def box_coords(box_index):
    return jnp.stack([box_index % 4, box_index // 4 % 2, box_index // 8], axis=1)


def arrange(key):
    box_key, slot_key, pair_key, offset_key, mix_key = jax.random.split(key, 5)
    box_order = jax.random.permutation(box_key, NB).astype(jnp.int32)
    slot_values = jax.random.permutation(slot_key, NB).astype(jnp.int32)
    places = jnp.arange(N, dtype=jnp.int32)
    owner_slot = slot_values[places // BLOCK]
    target = owner_slot % N_PROW * N_PCOL + places % BLOCK // (BLOCK // N_PCOL)
    grouped = jnp.argsort(target, stable=True).astype(jnp.int32).reshape(DEVICES, SRC)
    pair_count = SRC // CAP
    first_share = jax.random.randint(pair_key, (pair_count,), 0, CAP + 1).astype(jnp.int32).at[0].set(CAP)
    paired = jnp.stack([first_share, CAP - first_share], axis=1).reshape(2 * pair_count)
    offset_counts = jnp.concatenate([paired, jnp.zeros((DEVICES - 2 * pair_count,), jnp.int32)])
    shuffled = jax.random.permutation(offset_key, DEVICES).astype(jnp.int32)
    offsets = (shuffled - shuffled[0] + DEVICES // 2) % DEVICES
    bounds = jnp.cumsum(offset_counts)
    group_index = jnp.searchsorted(bounds, jnp.arange(SRC, dtype=jnp.int32), side='right')
    offset_each = offsets[group_index]
    source = (jnp.arange(DEVICES, dtype=jnp.int32)[:, None] + offset_each[None, :]) % DEVICES
    mixer = jax.random.permutation(mix_key, N).astype(jnp.int32)
    arrival = jnp.argsort(source.reshape(N) * N + mixer, stable=True)
    position = grouped.reshape(N)[arrival]
    return (box_order, slot_values, position)


def draw_samples(key, part):
    box_order, slot_values, position = arrange(key)
    key = jax.random.fold_in(key, 7)
    jitter_key = jax.random.fold_in(key, 0)
    spread = math.sqrt(2.0 * FEAT / 3.0)
    jitter = jax.random.uniform(jitter_key, (N, FEAT), jnp.float32, -1.0, 1.0)
    corner = box_coords(box_order[position // BLOCK]).astype(jnp.float32) * (0.5 * spread)
    shifted = jnp.concatenate([corner, jnp.zeros((N, FEAT - 3), jnp.float32)], axis=1)
    return jitter + shifted


def draw_position(key, part):
    layout = arrange(key)
    return layout[2]


def draw_slot_of_block(key, part):
    layout = arrange(key)
    return layout[1]


def draw_structure(key, part):
    layout = arrange(key)
    coords = box_coords(layout[0])
    distance = jnp.max(jnp.abs(coords[:, None, :] - coords[None, :, :]), axis=2)
    return (distance <= 2).astype(jnp.int32)


def setup_inputs(seed: int = 0) -> dict:
    arg_keys = jax.random.split(jax.random.key(seed), 5)
    samples = draw_samples(jax.random.fold_in(arg_keys[4], 71), 0)
    position = draw_position(jax.random.fold_in(arg_keys[4], 71), 0)
    slot_of_block = draw_slot_of_block(jax.random.fold_in(arg_keys[4], 71), 0)
    structure = draw_structure(jax.random.fold_in(arg_keys[4], 71), 0)
    return {"samples": samples, "position": position, "slot_of_block": slot_of_block, "structure": structure}


HIGHEST = lax.Precision.HIGHEST
NUGGET = 1.0

def support_radius(features):
    return 10.0 * math.sqrt(2.0 * features / 3.0)

def kernel_values(left_rows, right_rows, radius):
    left_norm = lax.optimization_barrier(jnp.sum(left_rows * left_rows, axis=1))[:, None]
    right_norm = lax.optimization_barrier(jnp.sum(right_rows * right_rows, axis=1))[None, :]
    inner_products = jnp.einsum('af,bf->ab', left_rows, right_rows, precision=HIGHEST)
    squared = jnp.maximum(left_norm + right_norm - 2.0 * inner_products, 0.0)
    scaled = jnp.sqrt(squared) / radius
    remain = jnp.maximum(1.0 - scaled, 0.0)
    return lax.integer_pow(remain, 35) * (35.0 * scaled + 1.0)

def inverse_lower(matrix):
    identity = jnp.eye(matrix.shape[0], dtype=matrix.dtype)
    lower_factor = jnp.linalg.cholesky(matrix)
    inverse = lax.linalg.triangular_solve(lower_factor, identity, left_side=True, lower=True)
    return (lower_factor, inverse)

def place_lower(product, lower_factor, block_ids, block_id):
    product = jnp.where((block_ids == block_id)[:, None, None], lower_factor[None], product)
    return jnp.where((block_ids < block_id)[:, None, None], 0.0, product)

def reference(samples, position, slot_of_block, structure):
    sample_count, features = samples.shape
    blocks_total = slot_of_block.shape[0]
    radius = support_radius(features)
    row_blocks = blocks_total // N_PROW
    col_blocks = blocks_total // N_PCOL
    points = jnp.zeros_like(samples).at[position].set(samples).reshape(blocks_total, BLOCK, features)
    block_order = jnp.arange(blocks_total, dtype=jnp.int32)
    block_at_slot = jnp.zeros(blocks_total, jnp.int32).at[slot_of_block].set(block_order)
    row_ids = block_at_slot[block_order % row_blocks * N_PROW + block_order // row_blocks]
    col_ids = block_at_slot[block_order % col_blocks * N_PCOL + block_order // col_blocks]
    weights = structure.astype(samples.dtype)
    identity = jnp.eye(BLOCK, dtype=samples.dtype)

    def column_of(block_ids, block_id):
        gathered = points[block_ids].reshape(-1, features)
        values = kernel_values(gathered, points[block_id], radius).reshape(blocks_total, BLOCK, BLOCK)
        values = values * weights[block_ids, block_id][:, None, None]
        return values + NUGGET * (block_ids == block_id).astype(samples.dtype)[:, None, None] * identity[None]
    diag_first = kernel_values(points[0], points[0], radius) * weights[0, 0] + NUGGET * identity
    lower_first, inverse_first = inverse_lower(diag_first)
    link_block = jnp.dot(kernel_values(points[1], points[0], radius) * weights[1, 0], inverse_first.T, precision=HIGHEST)
    diag_second = kernel_values(points[1], points[1], radius) * weights[1, 1] + NUGGET * identity
    diag_second = diag_second - jnp.dot(link_block, link_block.T, precision=HIGHEST)
    lower_second, inverse_second = inverse_lower(diag_second)

    def panels_of(block_ids):
        first_panel = jnp.einsum('kab,cb->kac', column_of(block_ids, 0), inverse_first, precision=HIGHEST)
        first_panel = place_lower(first_panel, lower_first, block_ids, 0)
        updated = column_of(block_ids, 1) - jnp.einsum('kab,cb->kac', first_panel, link_block, precision=HIGHEST)
        second = jnp.einsum('kab,cb->kac', updated, inverse_second, precision=HIGHEST)
        second = place_lower(second, lower_second, block_ids, 1)
        return (first_panel, second)
    row_first, row_second = panels_of(row_ids)
    col_first, col_second = panels_of(col_ids)
    col_points = points[col_ids].reshape(sample_count, features)

    def trailing_row(inputs):
        row_id, row_points, first_rows, second_rows = inputs
        values = kernel_values(row_points, col_points, radius).reshape(BLOCK, blocks_total, BLOCK)
        values = values * weights[row_id, col_ids][None, :, None]
        values = values + NUGGET * (col_ids == row_id).astype(samples.dtype)[None, :, None] * identity[:, None, :]
        values = values - jnp.einsum('ac,mbc->amb', first_rows, col_first, precision=HIGHEST)
        values = values - jnp.einsum('ac,mbc->amb', second_rows, col_second, precision=HIGHEST)
        kept_mask = (col_ids <= row_id) & (col_ids >= 2)
        return jnp.where(kept_mask[None, :, None], values, 0.0)
    trailing = lax.map(trailing_row, (row_ids, points[row_ids], row_first, row_second))
    panel_out = jnp.concatenate([row_first, row_second], axis=-1).reshape(sample_count, 2 * BLOCK)
    return (panel_out, trailing.reshape(sample_count, sample_count))
```

```python
import functools
import math

import jax
import jax.numpy as jnp
from jax import lax
from jax.experimental import pallas as pl
from jax.experimental.pallas import tpu as pltpu
from jax.sharding import PartitionSpec as P

BLOCK = 256
FEAT = 64
NBLK = 64
NR = 8
NC = 16
SRC = 128
SHARE = BLOCK // NC
ROWB = NBLK // NR
COLB = NBLK // NC
RADIUS = 10.0 * math.sqrt(2.0 * FEAT / 3.0)
F32 = jnp.float32
BF16 = jnp.bfloat16
I32 = jnp.int32
STEP = 64
HOP1 = 3 * NC + 8
NUGGET = 1.0
VMEM_LIMIT = 58 * 1024 * 1024
HIGHEST = lax.Precision.HIGHEST
MESH = pl.DeviceIdType.MESH
NT = (((1,), (1,)), ((), ()))
NN = (((1,), (0,)), ((), ()))


def iota(shape, axis):
    return lax.broadcasted_iota(I32, shape, axis)


def mm(a, b, dims=NN, precision=None):
    return lax.dot_general(a, b, dims, precision=precision, preferred_element_type=F32)


def pieces(x):
    h = x.astype(BF16)
    left = x - h.astype(F32)
    m = left.astype(BF16)
    return [h, m, (left - m.astype(F32)).astype(BF16)]


def exchange_kernel(
    samples_ref, position_ref, slot_ref, structure_ref,
    rows_ref, cols_ref, diag_ref, x0_ref, x1_ref, l_ref,
    buf1, recv1, buf2, recv2, chunk, dshare, cols_a, cols_l, inverses, whole, scratch, below_l, below_r,
    s1, r1, s2, r2, s4, r4, s5, r5, s6, r6, own,
):
    r = lax.axis_index("prow")
    c = lax.axis_index("pcol")
    source_row = lax.rem(c, NR)
    barrier = pltpu.get_barrier_semaphore()

    def greet(row, col):
        pl.semaphore_signal(barrier, inc=1, device_id=(row, col), device_id_type=MESH)

    for d in range(1, NR):
        greet(lax.rem(r + d, NR), c)
    for d in range(1, NC):
        greet(r, lax.rem(c + d, NC))

    place = position_ref[...]
    block = place >> 8
    share = (place & 255) >> 4
    in_block = (iota((NBLK, SRC), 0) == block).astype(F32)
    slots_row = jnp.broadcast_to(slot_ref[...].astype(F32), (8, NBLK))
    slot = mm(slots_row, in_block)[0:1].astype(I32)
    dest_row = slot & (NR - 1)
    row_in_share = (place & (SHARE - 1)) + 1
    earlier = (iota((SRC, SRC), 0) < iota((SRC, SRC), 1)).astype(F32)

    def buckets(count, target):
        hit = (iota((count, SRC), 0) == target).astype(F32)
        before = mm(hit, earlier)
        rank = jnp.sum(hit * before, axis=0, keepdims=True).astype(I32)
        return hit * (rank == 0).astype(F32), hit * (rank == 1).astype(F32), rank

    first, second, rank = buckets(SRC, dest_row * NC + share)
    leading = block < 2
    pair = jnp.where(leading, share * 2 + block, -1)
    first01, second01, rank01 = buckets(2 * NC, pair)
    doubled = pieces(jnp.concatenate([samples_ref[...], samples_ref[...]], axis=0))
    low128 = iota((SRC, SRC), 1) < FEAT
    onehot = jnp.concatenate([first, first01, second, second01], axis=0).astype(BF16)
    picked = mm(
        jnp.concatenate([onehot] * 3, axis=1), jnp.concatenate(doubled, axis=1), NT
    )
    half = SRC + 2 * NC
    data = jnp.where(iota((half, SRC), 1) < FEAT, picked[:half], picked[half:])
    to_row = (iota((NR, SRC), 0) == dest_row).astype(F32)
    lanes = iota((SRC, SRC), 0)
    tags = (lanes == share * 2 + rank).astype(F32) * ((slot >> 3) * SHARE + row_in_share).astype(F32)
    lane01 = jnp.where(leading, 2 * NC + pair * 2 + rank01, -1)
    tags01 = (lanes == lane01).astype(F32) * row_in_share.astype(F32)
    meta = mm(
        jnp.concatenate([to_row, jnp.ones((NR, SRC), F32)], axis=1),
        jnp.concatenate([tags, tags01], axis=1),
        NT,
    )
    for i in range(NR):
        buf1[i, 0:NC] = data[i * NC : (i + 1) * NC]
        buf1[i, NC : 3 * NC] = data[SRC:]
        buf1[i, 3 * NC : 3 * NC + 8] = jnp.broadcast_to(meta[i : i + 1], (8, SRC))

    pl.semaphore_wait(barrier, (NR - 1) + (NC - 1))

    first_hop = []
    for d in range(1, NR):
        to = lax.rem(r + d, NR)
        copy = pltpu.make_async_remote_copy(
            buf1.at[to], recv1.at[pl.ds(HOP1 * d, HOP1)], s1.at[d], r1.at[d],
            device_id=(to, c), device_id_type=MESH,
        )
        copy.start()
        first_hop.append(copy)
    recv1[0:HOP1] = buf1[r]
    for copy in first_hop:
        copy.wait_recv()

    def every(row):
        return recv1[pl.ds(row, NR, stride=HOP1), :]

    tag_rows = every(3 * NC)
    for q in range(NC):
        buf2[q, 0:8] = every(q)
        buf2[q, 8:16] = every(NC + 2 * q)
        buf2[q, 16:24] = every(NC + 2 * q + 1)
        buf2[q, 24:32] = tag_rows
    second_hop = []
    for d in range(1, NC):
        to = lax.rem(c + d, NC)
        copy = pltpu.make_async_remote_copy(
            buf2.at[to], recv2.at[d], s2.at[d], r2.at[d], device_id=(r, to), device_id_type=MESH
        )
        copy.start()
        second_hop.append(copy)
    recv2[0] = buf2[c]
    for copy in second_hop:
        copy.wait_recv()

    line = iota((8, SRC), 0)
    mine = jnp.where(line < 2, 2 * c + line, 2 * NC + 4 * c + line - 2)
    mine = (iota((8, SRC), 1) == mine) & (line < 6)
    tag = mm(mine.astype(F32), recv2[:, 24:32, :].reshape(SRC, SRC), NT).astype(I32)

    def settle(count, part, line):
        got = recv2[:, 8 * part : 8 * part + 8, :].reshape(SRC, SRC)
        turned = pltpu.roll(got, FEAT, 1)
        both = jnp.concatenate(
            [jnp.where(low128, got, turned), jnp.where(low128, turned, got)], axis=0
        )
        wanted = jnp.concatenate([tag[line : line + 1], tag[line + 1 : line + 2]], axis=1)
        onehot = (iota((count, 2 * SRC), 0) + 1 == wanted).astype(F32).astype(BF16)
        return mm(
            jnp.concatenate([onehot] * 3, axis=1), jnp.concatenate(pieces(both), axis=0), NN
        )

    low16 = iota((SHARE, SRC), 1) < FEAT
    dshare[...] = jnp.where(low16, settle(SHARE, 1, 2), settle(SHARE, 2, 4))
    my_rows = pl.ds(pl.multiple_of(c * SHARE, SHARE), SHARE)
    diag_copies = []
    for d in range(1, NC):
        copy = pltpu.make_async_remote_copy(
            dshare, diag_ref.at[my_rows, :], s6.at[d], r6.at[c],
            device_id=(r, lax.rem(c + d, NC)), device_id_type=MESH,
        )
        copy.start()
        diag_copies.append(copy)
    diag_ref[my_rows, :] = dshare[...]

    placed = settle(SRC, 0, 0)
    low64 = iota((64, SRC), 1) < FEAT
    chunk[...] = jnp.where(low64, placed[0:64], placed[64:128]).reshape(2, 2, SHARE, SRC)
    row_copies = []
    for d in range(1, NC):
        copy = pltpu.make_async_remote_copy(
            chunk, rows_ref.at[:, :, my_rows, :], s4.at[d], r4.at[c],
            device_id=(r, lax.rem(c + d, NC)), device_id_type=MESH,
        )
        copy.start()
        row_copies.append(copy)
    own_rows = pltpu.make_async_copy(chunk, rows_ref.at[:, :, my_rows, :], own.at[0])
    own_rows.start()

    def from_device(d):
        q = lax.rem(c + d, NC)
        return q, pl.ds(pl.multiple_of(q * SHARE, SHARE), SHARE)

    cols_a[...] = jnp.zeros_like(cols_a)
    cols_l[...] = jnp.zeros_like(cols_l)
    whole[...] = jnp.zeros_like(whole)
    below_l[...] = jnp.zeros_like(below_l)
    below_r[...] = jnp.zeros_like(below_r)
    for copy in first_hop + second_hop:
        copy.wait_send()
    for d in range(1, NC):
        q, spot = from_device(d)
        pltpu.make_async_copy(dshare, diag_ref.at[spot, :], r6.at[q]).wait()

    left0, right0 = point_operands(diag_ref[...], 0)
    left1, right1 = point_operands(diag_ref[...], 1)
    weight = structure_ref[1, 0].astype(F32)
    for i, j, left, right in ((0, 0, left0, right0), (1, 0, left1, right0), (1, 1, left1, right1)):
        l_ref[0:BLOCK, 0:BLOCK] = mm(left, right, NT)
        for s in range(0, BLOCK, STEP):
            value = kappa(l_ref[s : s + STEP, 0:BLOCK])
            if i == j:
                on = iota((STEP, BLOCK), 0) + s == iota((STEP, BLOCK), 1)
                value = jnp.where(on, value + NUGGET, value)
            else:
                value = value * weight
            for g in range(BLOCK // STEP):
                cols_a[j * (BLOCK // STEP) + g, i * BLOCK + s : i * BLOCK + s + STEP, :] = value[
                    :, g * STEP : (g + 1) * STEP
                ]

    col_half = lax.div(c, NR)

    def col_copy(d):
        return pltpu.make_async_remote_copy(
            rows_ref.at[:, col_half], cols_ref, s5.at[d], r5.at[0],
            device_id=(lax.rem(r + d, NR), c), device_id_type=MESH,
        )

    own_cols = pltpu.make_async_copy(rows_ref.at[:, col_half], cols_ref, own.at[1])

    def pass_columns():
        for d in range(1, NC):
            q, spot = from_device(d)
            pltpu.make_async_copy(chunk, rows_ref.at[:, :, spot, :], r4.at[q]).wait()
        own_rows.wait()

        @pl.when(source_row == r)
        def _():
            for d in range(1, NR):
                col_copy(d).start()
            own_cols.start()

    factor(cols_a, cols_l, inverses, whole, l_ref, scratch, below_l, below_r, pass_columns)
    high, rest = halves(whole[...])
    for x_ref, top, count in ((x0_ref, 0, 1), (x1_ref, BLOCK, 2)):
        for b in range(count):
            spot = (slice(top, top + BLOCK), slice(BLOCK * b, BLOCK * (b + 1)))
            base = 3 * BLOCK * b
            x_ref[:, base : base + BLOCK] = high[spot]
            x_ref[:, base + BLOCK : base + 2 * BLOCK] = high[spot]
            x_ref[:, base + 2 * BLOCK : base + 3 * BLOCK] = rest[spot]

    @pl.when(source_row == r)
    def _():
        for d in range(1, NR):
            col_copy(d).wait_send()
        own_cols.wait()

    @pl.when(source_row != r)
    def _():
        pltpu.make_async_copy(rows_ref.at[:, 0], cols_ref, r5.at[0]).wait()

    for copy in row_copies + diag_copies:
        copy.wait_send()


def exchange(samples, position, slots, structure):
    dma = pltpu.SemaphoreType.DMA
    vmem = pl.BlockSpec(memory_space=pltpu.VMEM)
    smem = pl.BlockSpec(memory_space=pltpu.SMEM)
    hbm = pl.BlockSpec(memory_space=pl.ANY)
    n2 = 2 * BLOCK
    steps = n2 // STEP
    return pl.pallas_call(
        exchange_kernel,
        out_shape=(
            jax.ShapeDtypeStruct((2, 2, BLOCK, 128), F32),
            jax.ShapeDtypeStruct((2, BLOCK, 128), F32),
            jax.ShapeDtypeStruct((BLOCK, 128), F32),
            jax.ShapeDtypeStruct((BLOCK, 3 * BLOCK), BF16),
            jax.ShapeDtypeStruct((BLOCK, 6 * BLOCK), BF16),
            jax.ShapeDtypeStruct((n2, n2), F32),
        ),
        in_specs=[vmem, vmem, vmem, smem],
        out_specs=(hbm, hbm, vmem, vmem, vmem, vmem),
        scratch_shapes=[
            pltpu.VMEM((NR, HOP1, 128), F32),
            pltpu.VMEM((NR * HOP1, 128), F32),
            pltpu.VMEM((NC, 32, 128), F32),
            pltpu.VMEM((NC, 32, 128), F32),
            pltpu.VMEM((2, 2, SHARE, 128), F32),
            pltpu.VMEM((SHARE, 128), F32),
            pltpu.VMEM((steps, n2, STEP), F32),
            pltpu.VMEM((steps, n2, STEP), F32),
            pltpu.VMEM((steps, STEP, STEP), F32),
            pltpu.VMEM((n2, n2), F32),
            pltpu.VMEM((160, 8, 128), F32),
            pltpu.VMEM((n2, 3 * STEP), BF16),
            pltpu.VMEM((n2, 3 * STEP), BF16),
            dma((NR,)), dma((NR,)), dma((NC,)), dma((NC,)),
            dma((NC,)), dma((NC,)), dma((NR,)), dma((1,)), dma((NC,)), dma((NC,)),
            dma((2,)),
        ],
        compiler_params=pltpu.CompilerParams(
            collective_id=0, has_side_effects=True, vmem_limit_bytes=VMEM_LIMIT
        ),
        name="exchange",
    )(samples, position, slots, structure)


def halves(x):
    high = x.astype(BF16)
    return high, (x - high.astype(F32)).astype(BF16)


def three_left(x):
    high, rest = halves(x)
    return jnp.concatenate([high, rest, high], axis=1)


def three_right(x, axis=1):
    high, rest = halves(x)
    return jnp.concatenate([high, high, rest], axis=axis)


def inverse_factor(block, scratch):
    size = block.shape[0]
    eye = (iota((size, size), 0) == iota((size, size), 1)).astype(F32)
    both = jnp.concatenate([block, eye], axis=1)
    count = size // 8
    wide = (8, 2 * size)
    tiles = [both[8 * t : 8 * t + 8, :] for t in range(count)]
    sub = iota(wide, 0)
    out = []
    used = [0]

    def put(value):
        at = used[0]
        used[0] += 1
        scratch[at] = value
        return lambda k: jnp.broadcast_to(scratch[at, k : k + 1, :], wide)

    def spread(q, p):
        return [jnp.broadcast_to(tiles[q][:, 8 * p + j : 8 * p + j + 1], wide) for j in range(8)]

    ahead = spread(0, 0)
    for p in range(count):
        cols = {q: (ahead if q == p else spread(q, p)) for q in range(p, count)}
        ahead = spread(p + 1, p + 1) if p + 1 < count else None
        pivots = jnp.ones(wide, F32)
        for j in range(0, 8, 2):
            at1, at2, row = put(cols[p][j]), put(cols[p][j + 1]), put(tiles[p])
            a, b, c = at1(j), at1(j + 1), at2(j + 1)
            det = a * c - b * b
            inv1 = pltpu.reciprocal(a, approx=True)
            inv1 = inv1 * (2.0 - a * inv1)
            inv_det = pltpu.reciprocal(det, approx=True)
            inv2 = (a * inv_det) * (2.0 - det * inv_det)
            ratio = b * inv1
            pivots = jnp.where(sub == j, a, jnp.where(sub == j + 1, det * inv1, pivots))

            def scaled(x1, x2):
                return x1 * inv1, (x2 - ratio * x1) * inv2

            row1, row2 = scaled(row(j), row(j + 1))
            rest = [scaled(at1(k), at2(k)) for k in range(j + 2, 8)]
            for q in range(p, count):
                g1 = cols[q][j]
                g2 = cols[q][j + 1] - g1 * ratio
                if q == p:
                    g1 = jnp.where(sub > j, g1, 0.0)
                    g2 = jnp.where(sub > j + 1, g2, 0.0)
                for (u1, u2), k in zip(rest, range(j + 2, 8)):
                    cols[q][k] = (cols[q][k] - g1 * u1) - g2 * u2
                if q == p + 1:
                    next1, next2 = put(cols[q][j]), put(cols[q][j + 1])
                    for k in range(8):
                        u1, u2 = scaled(next1(k), next2(k))
                        ahead[k] = (ahead[k] - g1 * u1) - g2 * u2
                tiles[q] = (tiles[q] - g1 * row1) - g2 * row2
        scale = lax.rsqrt(pivots)
        scale = scale * (1.5 - 0.5 * pivots * scale * scale)
        out.append((tiles[p] * scale)[:, size:])
    return jnp.concatenate(out, axis=0)


def factor(cols_a, cols_l, inverses, x_ref, l_ref, scratch, below_l, below_r, after_first):
    steps, n, _ = cols_a.shape

    def step(start, i, block):
        base = start * STEP
        following = lax.rem(i + 1, steps)
        there = pl.ds(pl.multiple_of(following * STEP, STEP), STEP)
        for j in range(max(start, 1), steps):
            taken = mm(below_l[base:, :], below_r[j * STEP : (j + 1) * STEP], NT)
            cols_a[j, base:, :] = cols_a[j, base:, :] - taken
        left = three_left(cols_a[i, base:, :])
        inverse = inverse_factor(block, scratch)
        inverses[i] = inverse
        below = mm(left, three_right(inverse), NT)
        on = iota((n - base, STEP), 0) + base - i * STEP >= iota((n - base, STEP), 1)
        below = jnp.where(on, below, 0.0)
        cols_l[i, base:, :] = below
        below_l[base:, :] = three_left(below)
        below_r[base:, :] = three_right(below)
        return cols_a[following, there, :] - mm(below_l[there, :], below_r[there, :], NT)

    block = cols_a[0, 0:STEP, :]
    for start in range(0, steps, 2):
        block = lax.fori_loop(start, start + 2, functools.partial(step, start), block)
        if start == 0:
            after_first()
    for i in range(steps):
        l_ref[:, i * STEP : (i + 1) * STEP] = cols_l[i]
        x_ref[i * STEP : (i + 1) * STEP, i * STEP : (i + 1) * STEP] = inverses[i]
    size = STEP
    while size < n:
        for o in range(0, n, 2 * size):
            m, e = o + size, o + 2 * size
            part = mm(three_left(l_ref[m:e, o:m]), three_right(x_ref[o:m, o:m], 0))
            x_ref[m:e, o:m] = -mm(three_left(x_ref[m:e, m:e]), three_right(part, 0))
        size *= 2


def point_operands(packed, half):
    low = iota(packed.shape, 1) < FEAT
    turned = pltpu.roll(packed, FEAT, 1)
    x = jnp.where(jnp.logical_xor(low, half == 1), packed, turned) * (1.0 / RADIUS)
    norm = 0.5 * jnp.sum(x * x, axis=1, keepdims=True)

    def split(v):
        h = v.astype(BF16).astype(F32)
        m = (v - h).astype(BF16).astype(F32)
        return h, m, v - h - m

    h, m, l = split(x)
    nh, nm, nl = split(norm)
    lane = iota(packed.shape, 1)
    norms = jnp.where(lane % 3 == 0, nh, jnp.where(lane % 3 == 1, nm, nl))
    left_tail = jnp.where(lane < 3, norms, jnp.where(lane < 6, 1.0, 0.0))
    right_tail = jnp.where(lane < 3, 1.0, jnp.where(lane < 6, norms, 0.0))
    left = [h, jnp.where(low, h, m), jnp.where(low, m, l), left_tail]
    right = [
        -2.0 * jnp.where(low, h, m),
        -2.0 * jnp.where(low, l, h),
        -2.0 * jnp.where(low, m, h),
        right_tail,
    ]
    return (
        jnp.concatenate([g.astype(BF16) for g in left], axis=1),
        jnp.concatenate([g.astype(BF16) for g in right], axis=1),
    )


def kappa(squared, weight=1.0):
    x = jnp.maximum(squared, 1e-30)
    t = x * lax.rsqrt(x)
    s = jnp.maximum(1.0 - t, 0.0)
    s2 = s * s
    s4 = s2 * s2
    s8 = s4 * s4
    s16 = s8 * s8
    s32 = s16 * s16
    return (s32 * (s2 * s)) * (36.0 * weight - (35.0 * weight) * s)


def panel_kernel(
    slot_ref, structure_ref, row0_ref, rows_ref, cols_ref, diag_ref, x0_ref, x1_ref, l_ref, panel_ref, trailing_ref,
    order, sorted_cols, diag_rights, rights, cols3, left_now, left_next, rows3, wide, a3, a3_b, dist, prod, sem,
):
    k = pl.program_id(0)
    r = lax.axis_index("prow")
    c = lax.axis_index("pcol")
    chunk = 32

    def tile(j):
        return slice(BLOCK * j, BLOCK * (j + 1))

    def values(ident, start, stop, source, target):
        for b in range(2):
            w = structure_ref[ident, b].astype(F32)
            base = 3 * b
            for s in range(start, stop, chunk):
                h, l = halves(kappa(source[s : s + chunk, tile(b)], w))
                target[s : s + chunk, tile(base)] = h
                target[s : s + chunk, tile(base + 1)] = l
                target[s : s + chunk, tile(base + 2)] = h

    def first_product(source):
        return mm(source[:, : 3 * BLOCK], x0_ref[...], NT)

    def second_product(source):
        return mm(source[...], x1_ref[...], NT)

    @pl.when(k == 0)
    def _():
        def place(b, carry):
            order[slot_ref[b]] = b
            return carry

        lax.fori_loop(0, NBLK, place, 0)
        keys = [order[NC * m + c] for m in range(COLB)]
        keys = [jnp.where(key < 2, NBLK + key, key) for key in keys]
        for m in range(COLB):
            rank = sum(jnp.where(other < keys[m], 1, 0) for other in keys)
            sorted_cols[rank] = m
        for b in range(2):
            diag_rights[tile(b), :] = point_operands(diag_ref[...], b)[1]
        wides = [
            buffer.at[:, 2 * BLOCK * g : 2 * BLOCK * (g + 1)] for buffer in (dist, prod) for g in range(2)
        ]
        for j in range(COLB):
            m = sorted_cols[j]
            left, right = point_operands(cols_ref[m % 2], m // 2)
            rights[tile(j), :] = right
            wides[j][...] = mm(left, diag_rights[...], NT)
        left = point_operands(row0_ref[0, 0], 0)[0]
        left_next[...] = left
        buffers = (a3, a3_b)
        for j in range(COLB):
            values(order[NC * sorted_cols[j] + c], 0, BLOCK, wides[j], buffers[j % 2])
            source = buffers[j % 2]
            for b, value in enumerate((first_product(source), second_product(source))):
                high, rest = halves(value)
                cols3[tile(j), tile(3 * b)] = high
                cols3[tile(j), tile(3 * b + 1)] = high
                cols3[tile(j), tile(3 * b + 2)] = rest
        wide[...] = mm(left, diag_rights[...], NT)

    past = order[NR * jnp.maximum(k - 1, 0) + r]
    ident = order[NR * jnp.minimum(k, ROWB - 1) + r]
    col_ids = [order[NC * sorted_cols[j] + c] for j in range(COLB)]
    kept = sum(jnp.where((col >= 2) & (col <= past), 1, 0) for col in col_ids)
    kept = jnp.where(k == 0, 0, kept)

    def spot(j):
        return pl.ds(pl.multiple_of(sorted_cols[j] * BLOCK, BLOCK), BLOCK)

    def step(count, last):
        def trail(j):
            w = structure_ref[past, col_ids[j]].astype(F32)
            for s in range(0, BLOCK, chunk):
                value = kappa(dist[s : s + chunk, tile(j)], w) - prod[s : s + chunk, tile(j)]
                trailing_ref[s : s + chunk, spot(j)] = value

        if count:
            here = slice(0, BLOCK * count)
            dist[:, here] = mm(left_now[...], rights[here, :], NT)
        quarter = BLOCK // COLB
        for j in range(COLB):
            if j < count:
                prod[:, tile(j)] = mm(rows3[...], cols3[tile(j), :], NT)
            if not last:
                values(ident, quarter * j, quarter * (j + 1), wide, a3)
        if not last:
            c0 = first_product(a3)
        for j in range(count // 2):
            trail(j)
        if not last:
            c1 = second_product(a3)
            left = point_operands(rows_ref[0, 0], jnp.minimum(k + 1, ROWB - 1) // 4)[0]
            wide[...] = mm(left, diag_rights[...], NT)
        for j in range(count // 2, count):
            trail(j)
        for j in range(count, COLB):
            trailing_ref[:, spot(j)] = jnp.zeros((BLOCK, BLOCK), F32)
        if last:
            return
        left_now[...] = left_next[...]
        left_next[...] = left
        for b, value in enumerate((c0, c1)):
            high, rest = halves(value)
            panel_ref[:, tile(b)] = value
            rows3[:, tile(3 * b)] = high
            rows3[:, tile(3 * b + 1)] = rest
            rows3[:, tile(3 * b + 2)] = high

    for count in range(COLB + 1):

        @pl.when((kept == count) & (k < ROWB))
        def _():
            step(count, False)

        @pl.when((kept == count) & (k == ROWB))
        def _():
            step(count, True)

    @pl.when((ident < 2) & (k < ROWB))
    def _():
        source = pl.ds(pl.multiple_of(ident * BLOCK, BLOCK), BLOCK)
        copy = pltpu.make_async_copy(l_ref.at[source, :], panel_ref, sem)
        copy.start()
        copy.wait()

    for j in range(COLB):

        @pl.when((col_ids[j] == past) & (past >= 2))
        def _():
            eye = iota((BLOCK, BLOCK), 0) == iota((BLOCK, BLOCK), 1)
            trailing_ref[:, spot(j)] = trailing_ref[:, spot(j)] + jnp.where(eye, NUGGET, 0.0)


def panels_and_trailing(slots, structure, rows, cols, diag, x0, x1, lower):
    smem = pl.BlockSpec(memory_space=pltpu.SMEM)
    n2 = 2 * BLOCK
    n4 = COLB * BLOCK

    def row_block(k):
        k = jnp.minimum(k + 1, ROWB - 1)
        return (k % 4) // 2, k % 2, 0, 0

    return pl.pallas_call(
        panel_kernel,
        grid=(ROWB + 1,),
        out_shape=(
            jax.ShapeDtypeStruct((ROWB * BLOCK, n2), F32),
            jax.ShapeDtypeStruct((ROWB * BLOCK, n4), F32),
        ),
        in_specs=[
            smem,
            smem,
            pl.BlockSpec((1, 1, BLOCK, 128), lambda k: (0, 0, 0, 0)),
            pl.BlockSpec((1, 1, BLOCK, 128), row_block),
            pl.BlockSpec((2, BLOCK, 128), lambda k: (0, 0, 0)),
            pl.BlockSpec((BLOCK, 128), lambda k: (0, 0)),
            pl.BlockSpec((BLOCK, 3 * BLOCK), lambda k: (0, 0)),
            pl.BlockSpec((BLOCK, 6 * BLOCK), lambda k: (0, 0)),
            pl.BlockSpec(memory_space=pl.ANY),
        ],
        out_specs=(
            pl.BlockSpec((BLOCK, n2), lambda k: (jnp.minimum(k, ROWB - 1), 0)),
            pl.BlockSpec((BLOCK, n4), lambda k: (jnp.maximum(k - 1, 0), 0)),
        ),
        scratch_shapes=[
            pltpu.SMEM((NBLK,), I32),
            pltpu.SMEM((COLB,), I32),
            pltpu.VMEM((n2, n2), BF16),
            pltpu.VMEM((n4, n2), BF16),
            pltpu.VMEM((n4, 3 * n2), BF16),
            pltpu.VMEM((BLOCK, n2), BF16),
            pltpu.VMEM((BLOCK, n2), BF16),
            pltpu.VMEM((BLOCK, 3 * n2), BF16),
            pltpu.VMEM((BLOCK, n2), F32),
            pltpu.VMEM((BLOCK, 3 * n2), BF16),
            pltpu.VMEM((BLOCK, 3 * n2), BF16),
            pltpu.VMEM((BLOCK, n4), F32),
            pltpu.VMEM((BLOCK, n4), F32),
            pltpu.SemaphoreType.DMA,
        ],
        compiler_params=pltpu.CompilerParams(vmem_limit_bytes=VMEM_LIMIT),
        name="panels",
    )(slots, structure, rows, rows, cols, diag, x0, x1, lower)


def shards(samples, position, slot_of_block, structure):
    parts = exchange(
        samples.T, position.reshape(1, SRC), slot_of_block.reshape(1, NBLK), structure
    )
    return panels_and_trailing(slot_of_block, structure, *parts)


def solution(mesh):
    in_specs = (P(("prow", "pcol"), None), P(("prow", "pcol")), P(), P())
    out_specs = (P("prow", None), P("prow", "pcol"))
    return jax.shard_map(shards, mesh=mesh, in_specs=in_specs, out_specs=out_specs, check_vma=False)
```

```python
import functools
import math

import jax
import jax.numpy as jnp
from jax import lax
from jax.experimental import pallas as pl
from jax.experimental.pallas import tpu as pltpu
from jax.sharding import PartitionSpec as P

BLOCK = 256
FEAT = 64
NBLK = 64
NR = 8
NC = 16
SRC = 128
SHARE = BLOCK // NC
ROWB = NBLK // NR
COLB = NBLK // NC
RADIUS = 10.0 * math.sqrt(2.0 * FEAT / 3.0)
F32 = jnp.float32
BF16 = jnp.bfloat16
I32 = jnp.int32
STEP = 64
HOP1 = 3 * NC + 8
NUGGET = 1.0
VMEM_LIMIT = 58 * 1024 * 1024
HIGHEST = lax.Precision.HIGHEST
MESH = pl.DeviceIdType.MESH
NT = (((1,), (1,)), ((), ()))
NN = (((1,), (0,)), ((), ()))


def iota(shape, axis):
    return lax.broadcasted_iota(I32, shape, axis)


def mm(a, b, dims=NN, precision=None):
    return lax.dot_general(a, b, dims, precision=precision, preferred_element_type=F32)


def pieces(x):
    h = x.astype(BF16)
    left = x - h.astype(F32)
    m = left.astype(BF16)
    return [h, m, (left - m.astype(F32)).astype(BF16)]


def exchange_kernel(
    samples_ref, position_ref, slot_ref, structure_ref,
    rows_ref, cols_ref, diag_ref, x0_out, x1_out, l_out,
    buf1, recv1, buf2, recv2, chunk, dshare, cols_a, cols_l, inverses, whole, scratch, below_l, below_r, l_ref, x0_ref, x1_ref,
    s1, r1, s2, r2, s4, r4, s5, r5, s6, r6, own,
):
    r = lax.axis_index("prow")
    c = lax.axis_index("pcol")
    source_row = lax.rem(c, NR)
    barrier = pltpu.get_barrier_semaphore()

    def greet(row, col):
        pl.semaphore_signal(barrier, inc=1, device_id=(row, col), device_id_type=MESH)

    for d in range(1, NR):
        greet(lax.rem(r + d, NR), c)
    for d in range(1, NC):
        greet(r, lax.rem(c + d, NC))

    place = position_ref[...]
    block = place >> 8
    share = (place & 255) >> 4
    in_block = (iota((NBLK, SRC), 0) == block).astype(F32)
    slots_row = jnp.broadcast_to(slot_ref[...].astype(F32), (8, NBLK))
    slot = mm(slots_row, in_block)[0:1].astype(I32)
    dest_row = slot & (NR - 1)
    row_in_share = (place & (SHARE - 1)) + 1
    earlier = (iota((SRC, SRC), 0) < iota((SRC, SRC), 1)).astype(F32)

    def buckets(count, target):
        hit = (iota((count, SRC), 0) == target).astype(F32)
        before = mm(hit, earlier)
        rank = jnp.sum(hit * before, axis=0, keepdims=True).astype(I32)
        return hit * (rank == 0).astype(F32), hit * (rank == 1).astype(F32), rank

    first, second, rank = buckets(SRC, dest_row * NC + share)
    leading = block < 2
    pair = jnp.where(leading, share * 2 + block, -1)
    first01, second01, rank01 = buckets(2 * NC, pair)
    doubled = pieces(jnp.concatenate([samples_ref[...], samples_ref[...]], axis=0))
    low128 = iota((SRC, SRC), 1) < FEAT
    onehot = jnp.concatenate([first, first01, second, second01], axis=0).astype(BF16)
    picked = mm(
        jnp.concatenate([onehot] * 3, axis=1), jnp.concatenate(doubled, axis=1), NT
    )
    half = SRC + 2 * NC
    data = jnp.where(iota((half, SRC), 1) < FEAT, picked[:half], picked[half:])
    to_row = (iota((NR, SRC), 0) == dest_row).astype(F32)
    lanes = iota((SRC, SRC), 0)
    tags = (lanes == share * 2 + rank).astype(F32) * ((slot >> 3) * SHARE + row_in_share).astype(F32)
    lane01 = jnp.where(leading, 2 * NC + pair * 2 + rank01, -1)
    tags01 = (lanes == lane01).astype(F32) * row_in_share.astype(F32)
    meta = mm(
        jnp.concatenate([to_row, jnp.ones((NR, SRC), F32)], axis=1),
        jnp.concatenate([tags, tags01], axis=1),
        NT,
    )
    for i in range(NR):
        buf1[i, 0:NC] = data[i * NC : (i + 1) * NC]
        buf1[i, NC : 3 * NC] = data[SRC:]
        buf1[i, 3 * NC : 3 * NC + 8] = jnp.broadcast_to(meta[i : i + 1], (8, SRC))

    pl.semaphore_wait(barrier, (NR - 1) + (NC - 1))

    first_hop = []
    for d in range(1, NR):
        to = lax.rem(r + d, NR)
        copy = pltpu.make_async_remote_copy(
            buf1.at[to], recv1.at[pl.ds(HOP1 * d, HOP1)], s1.at[d], r1.at[d],
            device_id=(to, c), device_id_type=MESH,
        )
        copy.start()
        first_hop.append(copy)
    recv1[0:HOP1] = buf1[r]
    for copy in first_hop:
        copy.wait_recv()

    def every(row):
        return recv1[pl.ds(row, NR, stride=HOP1), :]

    tag_rows = every(3 * NC)
    for q in range(NC):
        buf2[q, 0:8] = every(q)
        buf2[q, 8:16] = every(NC + 2 * q)
        buf2[q, 16:24] = every(NC + 2 * q + 1)
        buf2[q, 24:32] = tag_rows
    second_hop = []
    for d in range(1, NC):
        to = lax.rem(c + d, NC)
        copy = pltpu.make_async_remote_copy(
            buf2.at[to], recv2.at[d], s2.at[d], r2.at[d], device_id=(r, to), device_id_type=MESH
        )
        copy.start()
        second_hop.append(copy)
    recv2[0] = buf2[c]
    for copy in second_hop:
        copy.wait_recv()

    line = iota((8, SRC), 0)
    mine = jnp.where(line < 2, 2 * c + line, 2 * NC + 4 * c + line - 2)
    mine = (iota((8, SRC), 1) == mine) & (line < 6)
    tag = mm(mine.astype(F32), recv2[:, 24:32, :].reshape(SRC, SRC), NT).astype(I32)

    def settle(count, part, line):
        got = recv2[:, 8 * part : 8 * part + 8, :].reshape(SRC, SRC)
        turned = pltpu.roll(got, FEAT, 1)
        both = jnp.concatenate(
            [jnp.where(low128, got, turned), jnp.where(low128, turned, got)], axis=0
        )
        wanted = jnp.concatenate([tag[line : line + 1], tag[line + 1 : line + 2]], axis=1)
        onehot = (iota((count, 2 * SRC), 0) + 1 == wanted).astype(F32).astype(BF16)
        return mm(
            jnp.concatenate([onehot] * 3, axis=1), jnp.concatenate(pieces(both), axis=0), NN
        )

    low16 = iota((SHARE, SRC), 1) < FEAT
    dshare[...] = jnp.where(low16, settle(SHARE, 1, 2), settle(SHARE, 2, 4))
    my_rows = pl.ds(pl.multiple_of(c * SHARE, SHARE), SHARE)
    diag_copies = []
    for d in range(1, NC):
        copy = pltpu.make_async_remote_copy(
            dshare, diag_ref.at[my_rows, :], s6.at[d], r6.at[c],
            device_id=(r, lax.rem(c + d, NC)), device_id_type=MESH,
        )
        copy.start()
        diag_copies.append(copy)
    diag_ref[my_rows, :] = dshare[...]

    placed = settle(SRC, 0, 0)
    low64 = iota((64, SRC), 1) < FEAT
    chunk[...] = jnp.where(low64, placed[0:64], placed[64:128]).reshape(2, 2, SHARE, SRC)
    row_copies = []
    for d in range(1, NC):
        copy = pltpu.make_async_remote_copy(
            chunk, rows_ref.at[:, :, my_rows, :], s4.at[d], r4.at[c],
            device_id=(r, lax.rem(c + d, NC)), device_id_type=MESH,
        )
        copy.start()
        row_copies.append(copy)
    own_rows = pltpu.make_async_copy(chunk, rows_ref.at[:, :, my_rows, :], own.at[0])
    own_rows.start()

    def from_device(d):
        q = lax.rem(c + d, NC)
        return q, pl.ds(pl.multiple_of(q * SHARE, SHARE), SHARE)

    cols_a[...] = jnp.zeros_like(cols_a)
    cols_l[...] = jnp.zeros_like(cols_l)
    whole[...] = jnp.zeros_like(whole)
    below_l[...] = jnp.zeros_like(below_l)
    below_r[...] = jnp.zeros_like(below_r)
    for copy in first_hop + second_hop:
        copy.wait_send()
    for d in range(1, NC):
        q, spot = from_device(d)
        pltpu.make_async_copy(dshare, diag_ref.at[spot, :], r6.at[q]).wait()

    left0, right0 = point_operands(diag_ref[...], 0)
    left1, right1 = point_operands(diag_ref[...], 1)
    weight = structure_ref[1, 0].astype(F32)
    for i, j, left, right in ((0, 0, left0, right0), (1, 0, left1, right0), (1, 1, left1, right1)):
        l_ref[0:BLOCK, 0:BLOCK] = mm(left, right, NT)
        for s in range(0, BLOCK, STEP):
            value = kappa(l_ref[s : s + STEP, 0:BLOCK])
            if i == j:
                on = iota((STEP, BLOCK), 0) + s == iota((STEP, BLOCK), 1)
                value = jnp.where(on, value + NUGGET, value)
            else:
                value = value * weight
            for g in range(BLOCK // STEP):
                cols_a[j * (BLOCK // STEP) + g, i * BLOCK + s : i * BLOCK + s + STEP, :] = value[
                    :, g * STEP : (g + 1) * STEP
                ]

    col_half = lax.div(c, NR)

    def col_copy(d):
        return pltpu.make_async_remote_copy(
            rows_ref.at[:, col_half], cols_ref, s5.at[d], r5.at[0],
            device_id=(lax.rem(r + d, NR), c), device_id_type=MESH,
        )

    own_cols = pltpu.make_async_copy(rows_ref.at[:, col_half], cols_ref, own.at[1])

    def pass_columns():
        for d in range(1, NC):
            q, spot = from_device(d)
            pltpu.make_async_copy(chunk, rows_ref.at[:, :, spot, :], r4.at[q]).wait()
        own_rows.wait()

        @pl.when(source_row == r)
        def _():
            for d in range(1, NR):
                col_copy(d).start()
            own_cols.start()

    def keep(x_ref, at, top, b):
        high, rest = halves(whole[top : top + BLOCK, BLOCK * b : BLOCK * (b + 1)])
        x_ref[:, at : at + BLOCK] = high
        x_ref[:, at + BLOCK : at + 2 * BLOCK] = high
        x_ref[:, at + 2 * BLOCK : at + 3 * BLOCK] = rest

    wide = 3 * BLOCK
    leaving = [
        pltpu.make_async_copy(l_ref, l_out, own.at[2]),
        pltpu.make_async_copy(x0_ref, x0_out, own.at[3]),
        pltpu.make_async_copy(
            x1_ref.at[:, pl.ds(wide, wide)], x1_out.at[:, pl.ds(wide, wide)], own.at[4]
        ),
        pltpu.make_async_copy(x1_ref.at[:, pl.ds(0, wide)], x1_out.at[:, pl.ds(0, wide)], own.at[5]),
    ]

    def before_last():
        keep(x0_ref, 0, 0, 0)
        keep(x1_ref, wide, BLOCK, 1)
        leaving[1].start()
        leaving[2].start()

    factor(
        cols_a, cols_l, inverses, whole, l_ref, scratch, below_l, below_r,
        pass_columns, leaving[0].start, before_last,
    )
    keep(x1_ref, 0, BLOCK, 0)
    leaving[3].start()

    @pl.when(source_row == r)
    def _():
        for d in range(1, NR):
            col_copy(d).wait_send()
        own_cols.wait()

    @pl.when(source_row != r)
    def _():
        pltpu.make_async_copy(rows_ref.at[:, 0], cols_ref, r5.at[0]).wait()

    for copy in row_copies + diag_copies:
        copy.wait_send()
    for copy in leaving:
        copy.wait()


def exchange(samples, position, slots, structure):
    dma = pltpu.SemaphoreType.DMA
    vmem = pl.BlockSpec(memory_space=pltpu.VMEM)
    smem = pl.BlockSpec(memory_space=pltpu.SMEM)
    hbm = pl.BlockSpec(memory_space=pl.ANY)
    n2 = 2 * BLOCK
    steps = n2 // STEP
    return pl.pallas_call(
        exchange_kernel,
        out_shape=(
            jax.ShapeDtypeStruct((2, 2, BLOCK, 128), F32),
            jax.ShapeDtypeStruct((2, BLOCK, 128), F32),
            jax.ShapeDtypeStruct((BLOCK, 128), F32),
            jax.ShapeDtypeStruct((BLOCK, 3 * BLOCK), BF16),
            jax.ShapeDtypeStruct((BLOCK, 6 * BLOCK), BF16),
            jax.ShapeDtypeStruct((n2, n2), F32),
        ),
        in_specs=[vmem, vmem, vmem, smem],
        out_specs=(hbm, hbm, vmem, hbm, hbm, hbm),
        scratch_shapes=[
            pltpu.VMEM((NR, HOP1, 128), F32),
            pltpu.VMEM((NR * HOP1, 128), F32),
            pltpu.VMEM((NC, 32, 128), F32),
            pltpu.VMEM((NC, 32, 128), F32),
            pltpu.VMEM((2, 2, SHARE, 128), F32),
            pltpu.VMEM((SHARE, 128), F32),
            pltpu.VMEM((steps, n2, STEP), F32),
            pltpu.VMEM((steps, n2, STEP), F32),
            pltpu.VMEM((steps, STEP, STEP), F32),
            pltpu.VMEM((n2, n2), F32),
            pltpu.VMEM((160, 8, 128), F32),
            pltpu.VMEM((n2, 3 * STEP), BF16),
            pltpu.VMEM((n2, 3 * STEP), BF16),
            pltpu.VMEM((n2, n2), F32),
            pltpu.VMEM((BLOCK, 3 * BLOCK), BF16),
            pltpu.VMEM((BLOCK, 6 * BLOCK), BF16),
            dma((NR,)), dma((NR,)), dma((NC,)), dma((NC,)),
            dma((NC,)), dma((NC,)), dma((NR,)), dma((1,)), dma((NC,)), dma((NC,)),
            dma((6,)),
        ],
        compiler_params=pltpu.CompilerParams(
            collective_id=0, has_side_effects=True, vmem_limit_bytes=VMEM_LIMIT
        ),
        name="exchange",
    )(samples, position, slots, structure)


def halves(x):
    high = x.astype(BF16)
    return high, (x - high.astype(F32)).astype(BF16)


def three_left(x):
    high, rest = halves(x)
    return jnp.concatenate([high, rest, high], axis=1)


def three_right(x, axis=1):
    high, rest = halves(x)
    return jnp.concatenate([high, high, rest], axis=axis)


def inverse_factor(block, scratch):
    size = block.shape[0]
    eye = (iota((size, size), 0) == iota((size, size), 1)).astype(F32)
    both = jnp.concatenate([block, eye], axis=1)
    count = size // 8
    wide = (8, 2 * size)
    tiles = [both[8 * t : 8 * t + 8, :] for t in range(count)]
    sub = iota(wide, 0)
    out = []
    used = [0]

    def put(value):
        at = used[0]
        used[0] += 1
        scratch[at] = value
        return lambda k: jnp.broadcast_to(scratch[at, k : k + 1, :], wide)

    def spread(q, p):
        return [jnp.broadcast_to(tiles[q][:, 8 * p + j : 8 * p + j + 1], wide) for j in range(8)]

    ahead = spread(0, 0)
    for p in range(count):
        cols = {q: (ahead if q == p else spread(q, p)) for q in range(p, count)}
        ahead = spread(p + 1, p + 1) if p + 1 < count else None
        pivots = jnp.ones(wide, F32)
        for j in range(0, 8, 2):
            at1, at2, row = put(cols[p][j]), put(cols[p][j + 1]), put(tiles[p])
            a, b, c = at1(j), at1(j + 1), at2(j + 1)
            det = a * c - b * b
            inv1 = pltpu.reciprocal(a, approx=True)
            inv1 = inv1 * (2.0 - a * inv1)
            inv_det = pltpu.reciprocal(det, approx=True)
            inv2 = (a * inv_det) * (2.0 - det * inv_det)
            ratio = b * inv1
            pivots = jnp.where(sub == j, a, jnp.where(sub == j + 1, det * inv1, pivots))

            def scaled(x1, x2):
                return x1 * inv1, (x2 - ratio * x1) * inv2

            row1, row2 = scaled(row(j), row(j + 1))
            rest = [scaled(at1(k), at2(k)) for k in range(j + 2, 8)]
            for q in range(p, count):
                g1 = cols[q][j]
                g2 = cols[q][j + 1] - g1 * ratio
                if q == p:
                    g1 = jnp.where(sub > j, g1, 0.0)
                    g2 = jnp.where(sub > j + 1, g2, 0.0)
                for (u1, u2), k in zip(rest, range(j + 2, 8)):
                    cols[q][k] = (cols[q][k] - g1 * u1) - g2 * u2
                if q == p + 1:
                    next1, next2 = put(cols[q][j]), put(cols[q][j + 1])
                    for k in range(8):
                        u1, u2 = scaled(next1(k), next2(k))
                        ahead[k] = (ahead[k] - g1 * u1) - g2 * u2
                tiles[q] = (tiles[q] - g1 * row1) - g2 * row2
        scale = lax.rsqrt(pivots)
        scale = scale * (1.5 - 0.5 * pivots * scale * scale)
        out.append((tiles[p] * scale)[:, size:])
    return jnp.concatenate(out, axis=0)


def factor(
    cols_a, cols_l, inverses, x_ref, l_ref, scratch, below_l, below_r, after_first, after_lower, before_last
):
    steps, n, _ = cols_a.shape

    def step(start, i, block):
        base = start * STEP
        following = lax.rem(i + 1, steps)
        there = pl.ds(pl.multiple_of(following * STEP, STEP), STEP)
        for j in range(max(start, 1), steps):
            taken = mm(below_l[base:, :], below_r[j * STEP : (j + 1) * STEP], NT)
            cols_a[j, base:, :] = cols_a[j, base:, :] - taken
        left = three_left(cols_a[i, base:, :])
        inverse = inverse_factor(block, scratch)
        inverses[i] = inverse
        below = mm(left, three_right(inverse), NT)
        on = iota((n - base, STEP), 0) + base - i * STEP >= iota((n - base, STEP), 1)
        below = jnp.where(on, below, 0.0)
        cols_l[i, base:, :] = below
        below_l[base:, :] = three_left(below)
        below_r[base:, :] = three_right(below)
        return cols_a[following, there, :] - mm(below_l[there, :], below_r[there, :], NT)

    block = cols_a[0, 0:STEP, :]
    for start in range(0, steps, 2):
        block = lax.fori_loop(start, start + 2, functools.partial(step, start), block)
        if start == 0:
            after_first()
    for i in range(steps):
        l_ref[:, i * STEP : (i + 1) * STEP] = cols_l[i]
        x_ref[i * STEP : (i + 1) * STEP, i * STEP : (i + 1) * STEP] = inverses[i]
    after_lower()
    size = STEP
    while size < n:
        if 2 * size == n:
            before_last()
        for o in range(0, n, 2 * size):
            m, e = o + size, o + 2 * size
            part = mm(three_left(l_ref[m:e, o:m]), three_right(x_ref[o:m, o:m], 0))
            x_ref[m:e, o:m] = -mm(three_left(x_ref[m:e, m:e]), three_right(part, 0))
        size *= 2


def point_operands(packed, half):
    low = iota(packed.shape, 1) < FEAT
    turned = pltpu.roll(packed, FEAT, 1)
    x = jnp.where(jnp.logical_xor(low, half == 1), packed, turned) * (1.0 / RADIUS)
    norm = 0.5 * jnp.sum(x * x, axis=1, keepdims=True)

    def split(v):
        h = v.astype(BF16).astype(F32)
        m = (v - h).astype(BF16).astype(F32)
        return h, m, v - h - m

    h, m, l = split(x)
    nh, nm, nl = split(norm)
    lane = iota(packed.shape, 1)
    norms = jnp.where(lane % 3 == 0, nh, jnp.where(lane % 3 == 1, nm, nl))
    left_tail = jnp.where(lane < 3, norms, jnp.where(lane < 6, 1.0, 0.0))
    right_tail = jnp.where(lane < 3, 1.0, jnp.where(lane < 6, norms, 0.0))
    left = [h, jnp.where(low, h, m), jnp.where(low, m, l), left_tail]
    right = [
        -2.0 * jnp.where(low, h, m),
        -2.0 * jnp.where(low, l, h),
        -2.0 * jnp.where(low, m, h),
        right_tail,
    ]
    return (
        jnp.concatenate([g.astype(BF16) for g in left], axis=1),
        jnp.concatenate([g.astype(BF16) for g in right], axis=1),
    )


def kappa(squared, weight=1.0):
    x = jnp.maximum(squared, 1e-30)
    t = x * lax.rsqrt(x)
    s = jnp.maximum(1.0 - t, 0.0)
    s2 = s * s
    s4 = s2 * s2
    s8 = s4 * s4
    s16 = s8 * s8
    s32 = s16 * s16
    return (s32 * (s2 * s)) * (36.0 * weight - (35.0 * weight) * s)


def panel_kernel(
    slot_ref, structure_ref, row0_ref, rows_ref, cols_ref, diag_ref, x0_ref, x1_ref, l_ref, panel_ref, trailing_ref,
    order, sorted_cols, diag_rights, rights, cols3, left_now, left_next, rows3, wide, a3, a3_b, dist, prod, sem,
):
    k = pl.program_id(0)
    r = lax.axis_index("prow")
    c = lax.axis_index("pcol")
    chunk = 32

    def tile(j):
        return slice(BLOCK * j, BLOCK * (j + 1))

    def values(ident, start, stop, source, target):
        for b in range(2):
            w = structure_ref[ident, b].astype(F32)
            base = 3 * b
            for s in range(start, stop, chunk):
                h, l = halves(kappa(source[s : s + chunk, tile(b)], w))
                target[s : s + chunk, tile(base)] = h
                target[s : s + chunk, tile(base + 1)] = l
                target[s : s + chunk, tile(base + 2)] = h

    def first_product(source):
        return mm(source[:, : 3 * BLOCK], x0_ref[...], NT)

    def second_product(source):
        return mm(source[...], x1_ref[...], NT)

    @pl.when(k == 0)
    def _():
        def place(b, carry):
            order[slot_ref[b]] = b
            return carry

        lax.fori_loop(0, NBLK, place, 0)
        keys = [order[NC * m + c] for m in range(COLB)]
        keys = [jnp.where(key < 2, NBLK + key, key) for key in keys]
        for m in range(COLB):
            rank = sum(jnp.where(other < keys[m], 1, 0) for other in keys)
            sorted_cols[rank] = m
        for b in range(2):
            diag_rights[tile(b), :] = point_operands(diag_ref[...], b)[1]
        wides = [
            buffer.at[:, 2 * BLOCK * g : 2 * BLOCK * (g + 1)] for buffer in (dist, prod) for g in range(2)
        ]
        for j in range(COLB):
            m = sorted_cols[j]
            left, right = point_operands(cols_ref[m % 2], m // 2)
            rights[tile(j), :] = right
            wides[j][...] = mm(left, diag_rights[...], NT)
        left = point_operands(row0_ref[0, 0], 0)[0]
        left_next[...] = left
        buffers = (a3, a3_b)
        for j in range(COLB):
            values(order[NC * sorted_cols[j] + c], 0, BLOCK, wides[j], buffers[j % 2])
            source = buffers[j % 2]
            for b, value in enumerate((first_product(source), second_product(source))):
                high, rest = halves(value)
                cols3[tile(j), tile(3 * b)] = high
                cols3[tile(j), tile(3 * b + 1)] = high
                cols3[tile(j), tile(3 * b + 2)] = rest
        wide[...] = mm(left, diag_rights[...], NT)

    past = order[NR * jnp.maximum(k - 1, 0) + r]
    ident = order[NR * jnp.minimum(k, ROWB - 1) + r]
    col_ids = [order[NC * sorted_cols[j] + c] for j in range(COLB)]
    kept = sum(jnp.where((col >= 2) & (col <= past), 1, 0) for col in col_ids)
    kept = jnp.where(k == 0, 0, kept)

    def spot(j):
        return pl.ds(pl.multiple_of(sorted_cols[j] * BLOCK, BLOCK), BLOCK)

    def step(count, last):
        def trail(j):
            w = structure_ref[past, col_ids[j]].astype(F32)
            for s in range(0, BLOCK, chunk):
                value = kappa(dist[s : s + chunk, tile(j)], w) - prod[s : s + chunk, tile(j)]
                trailing_ref[s : s + chunk, spot(j)] = value

        if count:
            here = slice(0, BLOCK * count)
            dist[:, here] = mm(left_now[...], rights[here, :], NT)
        quarter = BLOCK // COLB
        for j in range(COLB):
            if j < count:
                prod[:, tile(j)] = mm(rows3[...], cols3[tile(j), :], NT)
            if not last:
                values(ident, quarter * j, quarter * (j + 1), wide, a3)
        if not last:
            c0 = first_product(a3)
        for j in range(count // 2):
            trail(j)
        if not last:
            c1 = second_product(a3)
            left = point_operands(rows_ref[0, 0], jnp.minimum(k + 1, ROWB - 1) // 4)[0]
            wide[...] = mm(left, diag_rights[...], NT)
        for j in range(count // 2, count):
            trail(j)
        for j in range(count, COLB):
            trailing_ref[:, spot(j)] = jnp.zeros((BLOCK, BLOCK), F32)
        if last:
            return
        left_now[...] = left_next[...]
        left_next[...] = left
        for b, value in enumerate((c0, c1)):
            high, rest = halves(value)
            panel_ref[:, tile(b)] = value
            rows3[:, tile(3 * b)] = high
            rows3[:, tile(3 * b + 1)] = rest
            rows3[:, tile(3 * b + 2)] = high

    for count in range(COLB + 1):

        @pl.when((kept == count) & (k < ROWB))
        def _():
            step(count, False)

        @pl.when((kept == count) & (k == ROWB))
        def _():
            step(count, True)

    @pl.when((ident < 2) & (k < ROWB))
    def _():
        source = pl.ds(pl.multiple_of(ident * BLOCK, BLOCK), BLOCK)
        copy = pltpu.make_async_copy(l_ref.at[source, :], panel_ref, sem)
        copy.start()
        copy.wait()

    for j in range(COLB):

        @pl.when((col_ids[j] == past) & (past >= 2))
        def _():
            eye = iota((BLOCK, BLOCK), 0) == iota((BLOCK, BLOCK), 1)
            trailing_ref[:, spot(j)] = trailing_ref[:, spot(j)] + jnp.where(eye, NUGGET, 0.0)


def panels_and_trailing(slots, structure, rows, cols, diag, x0, x1, lower):
    smem = pl.BlockSpec(memory_space=pltpu.SMEM)
    n2 = 2 * BLOCK
    n4 = COLB * BLOCK

    def row_block(k):
        k = jnp.minimum(k + 1, ROWB - 1)
        return (k % 4) // 2, k % 2, 0, 0

    return pl.pallas_call(
        panel_kernel,
        grid=(ROWB + 1,),
        out_shape=(
            jax.ShapeDtypeStruct((ROWB * BLOCK, n2), F32),
            jax.ShapeDtypeStruct((ROWB * BLOCK, n4), F32),
        ),
        in_specs=[
            smem,
            smem,
            pl.BlockSpec((1, 1, BLOCK, 128), lambda k: (0, 0, 0, 0)),
            pl.BlockSpec((1, 1, BLOCK, 128), row_block),
            pl.BlockSpec((2, BLOCK, 128), lambda k: (0, 0, 0)),
            pl.BlockSpec((BLOCK, 128), lambda k: (0, 0)),
            pl.BlockSpec((BLOCK, 3 * BLOCK), lambda k: (0, 0)),
            pl.BlockSpec((BLOCK, 6 * BLOCK), lambda k: (0, 0)),
            pl.BlockSpec(memory_space=pl.ANY),
        ],
        out_specs=(
            pl.BlockSpec((BLOCK, n2), lambda k: (jnp.minimum(k, ROWB - 1), 0)),
            pl.BlockSpec((BLOCK, n4), lambda k: (jnp.maximum(k - 1, 0), 0)),
        ),
        scratch_shapes=[
            pltpu.SMEM((NBLK,), I32),
            pltpu.SMEM((COLB,), I32),
            pltpu.VMEM((n2, n2), BF16),
            pltpu.VMEM((n4, n2), BF16),
            pltpu.VMEM((n4, 3 * n2), BF16),
            pltpu.VMEM((BLOCK, n2), BF16),
            pltpu.VMEM((BLOCK, n2), BF16),
            pltpu.VMEM((BLOCK, 3 * n2), BF16),
            pltpu.VMEM((BLOCK, n2), F32),
            pltpu.VMEM((BLOCK, 3 * n2), BF16),
            pltpu.VMEM((BLOCK, 3 * n2), BF16),
            pltpu.VMEM((BLOCK, n4), F32),
            pltpu.VMEM((BLOCK, n4), F32),
            pltpu.SemaphoreType.DMA,
        ],
        compiler_params=pltpu.CompilerParams(vmem_limit_bytes=VMEM_LIMIT),
        name="panels",
    )(slots, structure, rows, rows, cols, diag, x0, x1, lower)


def shards(samples, position, slot_of_block, structure):
    parts = exchange(
        samples.T, position.reshape(1, SRC), slot_of_block.reshape(1, NBLK), structure
    )
    return panels_and_trailing(slot_of_block, structure, *parts)


def solution(mesh):
    in_specs = (P(("prow", "pcol"), None), P(("prow", "pcol")), P(), P())
    out_specs = (P("prow", None), P("prow", "pcol"))
    return jax.shard_map(shards, mesh=mesh, in_specs=in_specs, out_specs=out_specs, check_vma=False)
```

```python
import functools
import math

import jax
import jax.numpy as jnp
from jax import lax
from jax.experimental import pallas as pl
from jax.experimental.pallas import tpu as pltpu
from jax.sharding import PartitionSpec as P

BLOCK = 256
FEAT = 64
NBLK = 64
NR = 8
NC = 16
SRC = 128
SHARE = BLOCK // NC
ROWB = NBLK // NR
COLB = NBLK // NC
RADIUS = 10.0 * math.sqrt(2.0 * FEAT / 3.0)
F32 = jnp.float32
BF16 = jnp.bfloat16
I32 = jnp.int32
STEP = 64
HOP1 = 3 * NC + 8
NUGGET = 1.0
VMEM_LIMIT = 58 * 1024 * 1024
HIGHEST = lax.Precision.HIGHEST
MESH = pl.DeviceIdType.MESH
NT = (((1,), (1,)), ((), ()))
NN = (((1,), (0,)), ((), ()))


def iota(shape, axis):
    return lax.broadcasted_iota(I32, shape, axis)


def mm(a, b, dims=NN, precision=None):
    return lax.dot_general(a, b, dims, precision=precision, preferred_element_type=F32)


def pieces(x):
    h = x.astype(BF16)
    left = x - h.astype(F32)
    m = left.astype(BF16)
    return [h, m, (left - m.astype(F32)).astype(BF16)]


def exchange_kernel(
    samples_ref, position_ref, slot_ref, structure_ref,
    rows_ref, cols_ref, diag_out, x0_out, x1_out, l_out,
    buf1, recv1, buf2, recv2, chunk, dshare, cols_a, cols_l, inverses, whole, scratch, below_l, below_r, l_ref, x0_ref, x1_ref, diag_ref,
    s1, r1, s2, r2, s4, r4, s5, r5, s6, r6, own,
):
    r = lax.axis_index("prow")
    c = lax.axis_index("pcol")
    source_row = lax.rem(c, NR)
    barrier = pltpu.get_barrier_semaphore()

    def greet(row, col):
        pl.semaphore_signal(barrier, inc=1, device_id=(row, col), device_id_type=MESH)

    for d in range(1, NR):
        greet(lax.rem(r + d, NR), c)
    for d in range(1, NC):
        greet(r, lax.rem(c + d, NC))

    place = position_ref[...]
    block = place >> 8
    share = (place & 255) >> 4
    in_block = (iota((NBLK, SRC), 0) == block).astype(F32)
    slots_row = jnp.broadcast_to(slot_ref[...].astype(F32), (8, NBLK))
    slot = mm(slots_row, in_block)[0:1].astype(I32)
    dest_row = slot & (NR - 1)
    row_in_share = (place & (SHARE - 1)) + 1
    earlier = (iota((SRC, SRC), 0) < iota((SRC, SRC), 1)).astype(F32)

    def buckets(count, target):
        hit = (iota((count, SRC), 0) == target).astype(F32)
        before = mm(hit, earlier)
        rank = jnp.sum(hit * before, axis=0, keepdims=True).astype(I32)
        return hit * (rank == 0).astype(F32), hit * (rank == 1).astype(F32), rank

    first, second, rank = buckets(SRC, dest_row * NC + share)
    leading = block < 2
    pair = jnp.where(leading, share * 2 + block, -1)
    first01, second01, rank01 = buckets(2 * NC, pair)
    doubled = pieces(jnp.concatenate([samples_ref[...], samples_ref[...]], axis=0))
    low128 = iota((SRC, SRC), 1) < FEAT
    onehot = jnp.concatenate([first, first01, second, second01], axis=0).astype(BF16)
    picked = mm(
        jnp.concatenate([onehot] * 3, axis=1), jnp.concatenate(doubled, axis=1), NT
    )
    half = SRC + 2 * NC
    data = jnp.where(iota((half, SRC), 1) < FEAT, picked[:half], picked[half:])
    to_row = (iota((NR, SRC), 0) == dest_row).astype(F32)
    lanes = iota((SRC, SRC), 0)
    tags = (lanes == share * 2 + rank).astype(F32) * ((slot >> 3) * SHARE + row_in_share).astype(F32)
    lane01 = jnp.where(leading, 2 * NC + pair * 2 + rank01, -1)
    tags01 = (lanes == lane01).astype(F32) * row_in_share.astype(F32)
    meta = mm(
        jnp.concatenate([to_row, jnp.ones((NR, SRC), F32)], axis=1),
        jnp.concatenate([tags, tags01], axis=1),
        NT,
    )
    for i in range(NR):
        buf1[i, 0:NC] = data[i * NC : (i + 1) * NC]
        buf1[i, NC : 3 * NC] = data[SRC:]
        buf1[i, 3 * NC : 3 * NC + 8] = jnp.broadcast_to(meta[i : i + 1], (8, SRC))

    pl.semaphore_wait(barrier, (NR - 1) + (NC - 1))

    first_hop = []
    for d in range(1, NR):
        to = lax.rem(r + d, NR)
        copy = pltpu.make_async_remote_copy(
            buf1.at[to], recv1.at[pl.ds(HOP1 * d, HOP1)], s1.at[d], r1.at[d],
            device_id=(to, c), device_id_type=MESH,
        )
        copy.start()
        first_hop.append(copy)
    recv1[0:HOP1] = buf1[r]
    for copy in first_hop:
        copy.wait_recv()

    def every(row):
        return recv1[pl.ds(row, NR, stride=HOP1), :]

    tag_rows = every(3 * NC)
    for q in range(NC):
        buf2[q, 0:8] = every(q)
        buf2[q, 8:16] = every(NC + 2 * q)
        buf2[q, 16:24] = every(NC + 2 * q + 1)
        buf2[q, 24:32] = tag_rows
    second_hop = []
    for d in range(1, NC):
        to = lax.rem(c + d, NC)
        copy = pltpu.make_async_remote_copy(
            buf2.at[to], recv2.at[d], s2.at[d], r2.at[d], device_id=(r, to), device_id_type=MESH
        )
        copy.start()
        second_hop.append(copy)
    recv2[0] = buf2[c]
    for copy in second_hop:
        copy.wait_recv()

    line = iota((8, SRC), 0)
    mine = jnp.where(line < 2, 2 * c + line, 2 * NC + 4 * c + line - 2)
    mine = (iota((8, SRC), 1) == mine) & (line < 6)
    tag = mm(mine.astype(F32), recv2[:, 24:32, :].reshape(SRC, SRC), NT).astype(I32)

    def settle(count, part, line):
        got = recv2[:, 8 * part : 8 * part + 8, :].reshape(SRC, SRC)
        turned = pltpu.roll(got, FEAT, 1)
        both = jnp.concatenate(
            [jnp.where(low128, got, turned), jnp.where(low128, turned, got)], axis=0
        )
        wanted = jnp.concatenate([tag[line : line + 1], tag[line + 1 : line + 2]], axis=1)
        onehot = (iota((count, 2 * SRC), 0) + 1 == wanted).astype(F32).astype(BF16)
        return mm(
            jnp.concatenate([onehot] * 3, axis=1), jnp.concatenate(pieces(both), axis=0), NN
        )

    low16 = iota((SHARE, SRC), 1) < FEAT
    dshare[...] = jnp.where(low16, settle(SHARE, 1, 2), settle(SHARE, 2, 4))
    my_rows = pl.ds(pl.multiple_of(c * SHARE, SHARE), SHARE)
    diag_copies = []
    for d in range(1, NC):
        copy = pltpu.make_async_remote_copy(
            dshare, diag_ref.at[my_rows, :], s6.at[d], r6.at[c],
            device_id=(r, lax.rem(c + d, NC)), device_id_type=MESH,
        )
        copy.start()
        diag_copies.append(copy)
    diag_ref[my_rows, :] = dshare[...]

    placed = settle(SRC, 0, 0)
    low64 = iota((64, SRC), 1) < FEAT
    chunk[...] = jnp.where(low64, placed[0:64], placed[64:128]).reshape(2, 2, SHARE, SRC)
    row_copies = []
    for d in range(1, NC):
        copy = pltpu.make_async_remote_copy(
            chunk, rows_ref.at[:, :, my_rows, :], s4.at[d], r4.at[c],
            device_id=(r, lax.rem(c + d, NC)), device_id_type=MESH,
        )
        copy.start()
        row_copies.append(copy)
    own_rows = pltpu.make_async_copy(chunk, rows_ref.at[:, :, my_rows, :], own.at[0])
    own_rows.start()

    def from_device(d):
        q = lax.rem(c + d, NC)
        return q, pl.ds(pl.multiple_of(q * SHARE, SHARE), SHARE)

    cols_a[...] = jnp.zeros_like(cols_a)
    cols_l[...] = jnp.zeros_like(cols_l)
    whole[...] = jnp.zeros_like(whole)
    below_l[...] = jnp.zeros_like(below_l)
    below_r[...] = jnp.zeros_like(below_r)
    for copy in first_hop + second_hop:
        copy.wait_send()
    for d in range(1, NC):
        q, spot = from_device(d)
        pltpu.make_async_copy(dshare, diag_ref.at[spot, :], r6.at[q]).wait()
    own_diag = pltpu.make_async_copy(diag_ref, diag_out, own.at[6])
    own_diag.start()

    left0, right0 = point_operands(diag_ref[...], 0)
    left1, right1 = point_operands(diag_ref[...], 1)
    weight = structure_ref[1, 0].astype(F32)
    for i, j, left, right in ((0, 0, left0, right0), (1, 0, left1, right0), (1, 1, left1, right1)):
        l_ref[0:BLOCK, 0:BLOCK] = mm(left, right, NT)
        for s in range(0, BLOCK, STEP):
            value = kappa(l_ref[s : s + STEP, 0:BLOCK])
            if i == j:
                on = iota((STEP, BLOCK), 0) + s == iota((STEP, BLOCK), 1)
                value = jnp.where(on, value + NUGGET, value)
            else:
                value = value * weight
            for g in range(BLOCK // STEP):
                cols_a[j * (BLOCK // STEP) + g, i * BLOCK + s : i * BLOCK + s + STEP, :] = value[
                    :, g * STEP : (g + 1) * STEP
                ]

    col_half = lax.div(c, NR)

    def col_copy(d):
        return pltpu.make_async_remote_copy(
            rows_ref.at[:, col_half], cols_ref, s5.at[d], r5.at[0],
            device_id=(lax.rem(r + d, NR), c), device_id_type=MESH,
        )

    own_cols = pltpu.make_async_copy(rows_ref.at[:, col_half], cols_ref, own.at[1])

    def pass_columns():
        for d in range(1, NC):
            q, spot = from_device(d)
            pltpu.make_async_copy(chunk, rows_ref.at[:, :, spot, :], r4.at[q]).wait()
        own_rows.wait()

        @pl.when(source_row == r)
        def _():
            for d in range(1, NR):
                col_copy(d).start()
            own_cols.start()

    def keep(x_ref, at, top, b):
        high, rest = halves(whole[top : top + BLOCK, BLOCK * b : BLOCK * (b + 1)])
        x_ref[:, at : at + BLOCK] = high
        x_ref[:, at + BLOCK : at + 2 * BLOCK] = high
        x_ref[:, at + 2 * BLOCK : at + 3 * BLOCK] = rest

    wide = 3 * BLOCK
    leaving = [
        pltpu.make_async_copy(l_ref, l_out, own.at[2]),
        pltpu.make_async_copy(x0_ref, x0_out, own.at[3]),
        pltpu.make_async_copy(
            x1_ref.at[:, pl.ds(wide, wide)], x1_out.at[:, pl.ds(wide, wide)], own.at[4]
        ),
        pltpu.make_async_copy(x1_ref.at[:, pl.ds(0, wide)], x1_out.at[:, pl.ds(0, wide)], own.at[5]),
    ]

    def before_last():
        keep(x0_ref, 0, 0, 0)
        keep(x1_ref, wide, BLOCK, 1)
        leaving[1].start()
        leaving[2].start()

    factor(
        cols_a, cols_l, inverses, whole, l_ref, scratch, below_l, below_r,
        pass_columns, leaving[0].start, before_last,
    )
    keep(x1_ref, 0, BLOCK, 0)
    leaving[3].start()

    @pl.when(source_row == r)
    def _():
        for d in range(1, NR):
            col_copy(d).wait_send()
        own_cols.wait()

    @pl.when(source_row != r)
    def _():
        pltpu.make_async_copy(rows_ref.at[:, 0], cols_ref, r5.at[0]).wait()

    for copy in row_copies + diag_copies:
        copy.wait_send()
    for copy in [*leaving, own_diag]:
        copy.wait()


def exchange(samples, position, slots, structure):
    dma = pltpu.SemaphoreType.DMA
    vmem = pl.BlockSpec(memory_space=pltpu.VMEM)
    smem = pl.BlockSpec(memory_space=pltpu.SMEM)
    hbm = pl.BlockSpec(memory_space=pl.ANY)
    n2 = 2 * BLOCK
    steps = n2 // STEP
    return pl.pallas_call(
        exchange_kernel,
        out_shape=(
            jax.ShapeDtypeStruct((2, 2, BLOCK, 128), F32),
            jax.ShapeDtypeStruct((2, BLOCK, 128), F32),
            jax.ShapeDtypeStruct((BLOCK, 128), F32),
            jax.ShapeDtypeStruct((BLOCK, 3 * BLOCK), BF16),
            jax.ShapeDtypeStruct((BLOCK, 6 * BLOCK), BF16),
            jax.ShapeDtypeStruct((n2, n2), F32),
        ),
        in_specs=[vmem, vmem, vmem, smem],
        out_specs=(hbm,) * 6,
        scratch_shapes=[
            pltpu.VMEM((NR, HOP1, 128), F32),
            pltpu.VMEM((NR * HOP1, 128), F32),
            pltpu.VMEM((NC, 32, 128), F32),
            pltpu.VMEM((NC, 32, 128), F32),
            pltpu.VMEM((2, 2, SHARE, 128), F32),
            pltpu.VMEM((SHARE, 128), F32),
            pltpu.VMEM((steps, n2, STEP), F32),
            pltpu.VMEM((steps, n2, STEP), F32),
            pltpu.VMEM((steps, STEP, STEP), F32),
            pltpu.VMEM((n2, n2), F32),
            pltpu.VMEM((160, 8, 128), F32),
            pltpu.VMEM((n2, 3 * STEP), BF16),
            pltpu.VMEM((n2, 3 * STEP), BF16),
            pltpu.VMEM((n2, n2), F32),
            pltpu.VMEM((BLOCK, 3 * BLOCK), BF16),
            pltpu.VMEM((BLOCK, 6 * BLOCK), BF16),
            pltpu.VMEM((BLOCK, 128), F32),
            dma((NR,)), dma((NR,)), dma((NC,)), dma((NC,)),
            dma((NC,)), dma((NC,)), dma((NR,)), dma((1,)), dma((NC,)), dma((NC,)),
            dma((7,)),
        ],
        compiler_params=pltpu.CompilerParams(
            collective_id=0, has_side_effects=True, vmem_limit_bytes=VMEM_LIMIT
        ),
        name="exchange",
    )(samples, position, slots, structure)


def halves(x):
    high = x.astype(BF16)
    return high, (x - high.astype(F32)).astype(BF16)


def three_left(x):
    high, rest = halves(x)
    return jnp.concatenate([high, rest, high], axis=1)


def three_right(x, axis=1):
    high, rest = halves(x)
    return jnp.concatenate([high, high, rest], axis=axis)


def inverse_factor(block, scratch):
    size = block.shape[0]
    eye = (iota((size, size), 0) == iota((size, size), 1)).astype(F32)
    both = jnp.concatenate([block, eye], axis=1)
    count = size // 8
    wide = (8, 2 * size)
    tiles = [both[8 * t : 8 * t + 8, :] for t in range(count)]
    sub = iota(wide, 0)
    out = []
    used = [0]

    def put(value):
        at = used[0]
        used[0] += 1
        scratch[at] = value
        return lambda k: jnp.broadcast_to(scratch[at, k : k + 1, :], wide)

    def spread(q, p):
        return [jnp.broadcast_to(tiles[q][:, 8 * p + j : 8 * p + j + 1], wide) for j in range(8)]

    ahead = spread(0, 0)
    for p in range(count):
        cols = {q: (ahead if q == p else spread(q, p)) for q in range(p, count)}
        ahead = spread(p + 1, p + 1) if p + 1 < count else None
        pivots = jnp.ones(wide, F32)
        for j in range(0, 8, 2):
            at1, at2, row = put(cols[p][j]), put(cols[p][j + 1]), put(tiles[p])
            a, b, c = at1(j), at1(j + 1), at2(j + 1)
            det = a * c - b * b
            inv1 = pltpu.reciprocal(a, approx=True)
            inv1 = inv1 * (2.0 - a * inv1)
            inv_det = pltpu.reciprocal(det, approx=True)
            inv2 = (a * inv_det) * (2.0 - det * inv_det)
            ratio = b * inv1
            pivots = jnp.where(sub == j, a, jnp.where(sub == j + 1, det * inv1, pivots))

            def scaled(x1, x2):
                return x1 * inv1, (x2 - ratio * x1) * inv2

            row1, row2 = scaled(row(j), row(j + 1))
            rest = [scaled(at1(k), at2(k)) for k in range(j + 2, 8)]
            for q in range(p, count):
                g1 = cols[q][j]
                g2 = cols[q][j + 1] - g1 * ratio
                if q == p:
                    g1 = jnp.where(sub > j, g1, 0.0)
                    g2 = jnp.where(sub > j + 1, g2, 0.0)
                for (u1, u2), k in zip(rest, range(j + 2, 8)):
                    cols[q][k] = (cols[q][k] - g1 * u1) - g2 * u2
                if q == p + 1:
                    next1, next2 = put(cols[q][j]), put(cols[q][j + 1])
                    for k in range(8):
                        u1, u2 = scaled(next1(k), next2(k))
                        ahead[k] = (ahead[k] - g1 * u1) - g2 * u2
                tiles[q] = (tiles[q] - g1 * row1) - g2 * row2
        scale = lax.rsqrt(pivots)
        scale = scale * (1.5 - 0.5 * pivots * scale * scale)
        out.append((tiles[p] * scale)[:, size:])
    return jnp.concatenate(out, axis=0)


def factor(
    cols_a, cols_l, inverses, x_ref, l_ref, scratch, below_l, below_r, after_first, after_lower, before_last
):
    steps, n, _ = cols_a.shape

    def step(start, i, block):
        base = start * STEP
        following = lax.rem(i + 1, steps)
        there = pl.ds(pl.multiple_of(following * STEP, STEP), STEP)
        for j in range(max(start, 1), steps):
            taken = mm(below_l[base:, :], below_r[j * STEP : (j + 1) * STEP], NT)
            cols_a[j, base:, :] = cols_a[j, base:, :] - taken
        left = three_left(cols_a[i, base:, :])
        inverse = inverse_factor(block, scratch)
        inverses[i] = inverse
        below = mm(left, three_right(inverse), NT)
        on = iota((n - base, STEP), 0) + base - i * STEP >= iota((n - base, STEP), 1)
        below = jnp.where(on, below, 0.0)
        cols_l[i, base:, :] = below
        below_l[base:, :] = three_left(below)
        below_r[base:, :] = three_right(below)
        return cols_a[following, there, :] - mm(below_l[there, :], below_r[there, :], NT)

    block = cols_a[0, 0:STEP, :]
    for start in range(0, steps, 2):
        block = lax.fori_loop(start, start + 2, functools.partial(step, start), block)
        if start == 0:
            after_first()
    for i in range(steps):
        l_ref[:, i * STEP : (i + 1) * STEP] = cols_l[i]
        x_ref[i * STEP : (i + 1) * STEP, i * STEP : (i + 1) * STEP] = inverses[i]
    after_lower()
    size = STEP
    while size < n:
        if 2 * size == n:
            before_last()
        for o in range(0, n, 2 * size):
            m, e = o + size, o + 2 * size
            part = mm(three_left(l_ref[m:e, o:m]), three_right(x_ref[o:m, o:m], 0))
            x_ref[m:e, o:m] = -mm(three_left(x_ref[m:e, m:e]), three_right(part, 0))
        size *= 2


def point_operands(packed, half):
    low = iota(packed.shape, 1) < FEAT
    turned = pltpu.roll(packed, FEAT, 1)
    x = jnp.where(jnp.logical_xor(low, half == 1), packed, turned) * (1.0 / RADIUS)
    norm = 0.5 * jnp.sum(x * x, axis=1, keepdims=True)

    def split(v):
        h = v.astype(BF16).astype(F32)
        m = (v - h).astype(BF16).astype(F32)
        return h, m, v - h - m

    h, m, l = split(x)
    nh, nm, nl = split(norm)
    lane = iota(packed.shape, 1)
    norms = jnp.where(lane % 3 == 0, nh, jnp.where(lane % 3 == 1, nm, nl))
    left_tail = jnp.where(lane < 3, norms, jnp.where(lane < 6, 1.0, 0.0))
    right_tail = jnp.where(lane < 3, 1.0, jnp.where(lane < 6, norms, 0.0))
    left = [h, jnp.where(low, h, m), jnp.where(low, m, l), left_tail]
    right = [
        -2.0 * jnp.where(low, h, m),
        -2.0 * jnp.where(low, l, h),
        -2.0 * jnp.where(low, m, h),
        right_tail,
    ]
    return (
        jnp.concatenate([g.astype(BF16) for g in left], axis=1),
        jnp.concatenate([g.astype(BF16) for g in right], axis=1),
    )


def kappa(squared, weight=1.0):
    x = jnp.maximum(squared, 1e-30)
    t = x * lax.rsqrt(x)
    s = jnp.maximum(1.0 - t, 0.0)
    s2 = s * s
    s4 = s2 * s2
    s8 = s4 * s4
    s16 = s8 * s8
    s32 = s16 * s16
    return (s32 * (s2 * s)) * (36.0 * weight - (35.0 * weight) * s)


def panel_kernel(
    slot_ref, structure_ref, row0_ref, rows_ref, cols_ref, diag_ref, x0_ref, x1_ref, l_ref, panel_ref, trailing_ref,
    order, sorted_cols, diag_rights, rights, cols3, left_now, left_next, rows3, wide, a3, a3_b, dist, prod, sem,
):
    k = pl.program_id(0)
    r = lax.axis_index("prow")
    c = lax.axis_index("pcol")
    chunk = 32

    def tile(j):
        return slice(BLOCK * j, BLOCK * (j + 1))

    def values(ident, start, stop, source, target):
        for b in range(2):
            w = structure_ref[ident, b].astype(F32)
            base = 3 * b
            for s in range(start, stop, chunk):
                h, l = halves(kappa(source[s : s + chunk, tile(b)], w))
                target[s : s + chunk, tile(base)] = h
                target[s : s + chunk, tile(base + 1)] = l
                target[s : s + chunk, tile(base + 2)] = h

    def first_product(source):
        return mm(source[:, : 3 * BLOCK], x0_ref[...], NT)

    def second_product(source):
        return mm(source[...], x1_ref[...], NT)

    @pl.when(k == 0)
    def _():
        def place(b, carry):
            order[slot_ref[b]] = b
            return carry

        lax.fori_loop(0, NBLK, place, 0)
        keys = [order[NC * m + c] for m in range(COLB)]
        keys = [jnp.where(key < 2, NBLK + key, key) for key in keys]
        for m in range(COLB):
            rank = sum(jnp.where(other < keys[m], 1, 0) for other in keys)
            sorted_cols[rank] = m
        for b in range(2):
            diag_rights[tile(b), :] = point_operands(diag_ref[...], b)[1]
        wides = [
            buffer.at[:, 2 * BLOCK * g : 2 * BLOCK * (g + 1)] for buffer in (dist, prod) for g in range(2)
        ]
        for j in range(COLB):
            m = sorted_cols[j]
            left, right = point_operands(cols_ref[m % 2], m // 2)
            rights[tile(j), :] = right
            wides[j][...] = mm(left, diag_rights[...], NT)
        left = point_operands(row0_ref[0, 0], 0)[0]
        left_next[...] = left
        buffers = (a3, a3_b)
        for j in range(COLB):
            values(order[NC * sorted_cols[j] + c], 0, BLOCK, wides[j], buffers[j % 2])
            source = buffers[j % 2]
            for b, value in enumerate((first_product(source), second_product(source))):
                high, rest = halves(value)
                cols3[tile(j), tile(3 * b)] = high
                cols3[tile(j), tile(3 * b + 1)] = high
                cols3[tile(j), tile(3 * b + 2)] = rest
        wide[...] = mm(left, diag_rights[...], NT)

    past = order[NR * jnp.maximum(k - 1, 0) + r]
    ident = order[NR * jnp.minimum(k, ROWB - 1) + r]
    col_ids = [order[NC * sorted_cols[j] + c] for j in range(COLB)]
    kept = sum(jnp.where((col >= 2) & (col <= past), 1, 0) for col in col_ids)
    kept = jnp.where(k == 0, 0, kept)

    def spot(j):
        return pl.ds(pl.multiple_of(sorted_cols[j] * BLOCK, BLOCK), BLOCK)

    def step(count, last):
        def trail(j):
            w = structure_ref[past, col_ids[j]].astype(F32)
            for s in range(0, BLOCK, chunk):
                value = kappa(dist[s : s + chunk, tile(j)], w) - prod[s : s + chunk, tile(j)]
                trailing_ref[s : s + chunk, spot(j)] = value

        if count:
            here = slice(0, BLOCK * count)
            dist[:, here] = mm(left_now[...], rights[here, :], NT)
        quarter = BLOCK // COLB
        for j in range(COLB):
            if j < count:
                prod[:, tile(j)] = mm(rows3[...], cols3[tile(j), :], NT)
            if not last:
                values(ident, quarter * j, quarter * (j + 1), wide, a3)
        if not last:
            c0 = first_product(a3)
        for j in range(count // 2):
            trail(j)
        if not last:
            c1 = second_product(a3)
            left = point_operands(rows_ref[0, 0], jnp.minimum(k + 1, ROWB - 1) // 4)[0]
            wide[...] = mm(left, diag_rights[...], NT)
        for j in range(count // 2, count):
            trail(j)
        for j in range(count, COLB):
            trailing_ref[:, spot(j)] = jnp.zeros((BLOCK, BLOCK), F32)
        if last:
            return
        left_now[...] = left_next[...]
        left_next[...] = left
        for b, value in enumerate((c0, c1)):
            high, rest = halves(value)
            panel_ref[:, tile(b)] = value
            rows3[:, tile(3 * b)] = high
            rows3[:, tile(3 * b + 1)] = rest
            rows3[:, tile(3 * b + 2)] = high

    for count in range(COLB + 1):

        @pl.when((kept == count) & (k < ROWB))
        def _():
            step(count, False)

        @pl.when((kept == count) & (k == ROWB))
        def _():
            step(count, True)

    @pl.when((ident < 2) & (k < ROWB))
    def _():
        source = pl.ds(pl.multiple_of(ident * BLOCK, BLOCK), BLOCK)
        copy = pltpu.make_async_copy(l_ref.at[source, :], panel_ref, sem)
        copy.start()
        copy.wait()

    for j in range(COLB):

        @pl.when((col_ids[j] == past) & (past >= 2))
        def _():
            eye = iota((BLOCK, BLOCK), 0) == iota((BLOCK, BLOCK), 1)
            trailing_ref[:, spot(j)] = trailing_ref[:, spot(j)] + jnp.where(eye, NUGGET, 0.0)


def panels_and_trailing(slots, structure, rows, cols, diag, x0, x1, lower):
    smem = pl.BlockSpec(memory_space=pltpu.SMEM)
    n2 = 2 * BLOCK
    n4 = COLB * BLOCK

    def row_block(k):
        k = jnp.minimum(k + 1, ROWB - 1)
        return (k % 4) // 2, k % 2, 0, 0

    return pl.pallas_call(
        panel_kernel,
        grid=(ROWB + 1,),
        out_shape=(
            jax.ShapeDtypeStruct((ROWB * BLOCK, n2), F32),
            jax.ShapeDtypeStruct((ROWB * BLOCK, n4), F32),
        ),
        in_specs=[
            smem,
            smem,
            pl.BlockSpec((1, 1, BLOCK, 128), lambda k: (0, 0, 0, 0)),
            pl.BlockSpec((1, 1, BLOCK, 128), row_block),
            pl.BlockSpec((2, BLOCK, 128), lambda k: (0, 0, 0)),
            pl.BlockSpec((BLOCK, 128), lambda k: (0, 0)),
            pl.BlockSpec((BLOCK, 3 * BLOCK), lambda k: (0, 0)),
            pl.BlockSpec((BLOCK, 6 * BLOCK), lambda k: (0, 0)),
            pl.BlockSpec(memory_space=pl.ANY),
        ],
        out_specs=(
            pl.BlockSpec((BLOCK, n2), lambda k: (jnp.minimum(k, ROWB - 1), 0)),
            pl.BlockSpec((BLOCK, n4), lambda k: (jnp.maximum(k - 1, 0), 0)),
        ),
        scratch_shapes=[
            pltpu.SMEM((NBLK,), I32),
            pltpu.SMEM((COLB,), I32),
            pltpu.VMEM((n2, n2), BF16),
            pltpu.VMEM((n4, n2), BF16),
            pltpu.VMEM((n4, 3 * n2), BF16),
            pltpu.VMEM((BLOCK, n2), BF16),
            pltpu.VMEM((BLOCK, n2), BF16),
            pltpu.VMEM((BLOCK, 3 * n2), BF16),
            pltpu.VMEM((BLOCK, n2), F32),
            pltpu.VMEM((BLOCK, 3 * n2), BF16),
            pltpu.VMEM((BLOCK, 3 * n2), BF16),
            pltpu.VMEM((BLOCK, n4), F32),
            pltpu.VMEM((BLOCK, n4), F32),
            pltpu.SemaphoreType.DMA,
        ],
        compiler_params=pltpu.CompilerParams(vmem_limit_bytes=VMEM_LIMIT),
        name="panels",
    )(slots, structure, rows, rows, cols, diag, x0, x1, lower)


def shards(samples, position, slot_of_block, structure):
    parts = exchange(
        samples.T, position.reshape(1, SRC), slot_of_block.reshape(1, NBLK), structure
    )
    return panels_and_trailing(slot_of_block, structure, *parts)


def solution(mesh):
    in_specs = (P(("prow", "pcol"), None), P(("prow", "pcol")), P(), P())
    out_specs = (P("prow", None), P("prow", "pcol"))
    return jax.shard_map(shards, mesh=mesh, in_specs=in_specs, out_specs=out_specs, check_vma=False)
```
